32 devices in a mesh: groups: 2 (over x), goal: 16 (over z, y, core).
Axes of the slice: x: 2, y: 2, z: 4, core: 2. Of those that a mesh axis runs over, the one named last changes fastest.
Arguments:
- queries: bfloat16 [128, 64, 4096], P(('groups', 'goal')), parts along dimension 0, may hold values from -8 to 8
- goal_keys: bfloat16 [32, 256, 4096], P(('groups', 'goal')), parts along dimension 0, may hold values from -8 to 8
- goal_values: bfloat16 [32, 256, 4096], P(('groups', 'goal')), parts along dimension 0, may hold values from -6 to 6
- out_weight: bfloat16 [4096, 2048], P('goal'), may hold values from -0.5 to 0.5
- tactic_goal: int32 [128, 1], P(('groups', 'goal')), parts along dimension 0, may hold values from 0 to 15
- tactic_len: int32 [128], P(('groups', 'goal')), parts along dimension 0, may hold values from 1 to 64
Outputs:
- projected: bfloat16 [128, 64, 2048], P(('groups', 'goal')), parts along dimension 0
The draws below stay inside these ranges and needn't reach their ends.
There are 2 independent parts, one for each index of `groups`. The reference program is written for one: setup_inputs(seed, part) draws one part's arguments, and reference() takes and returns one part's arrays. A program takes and returns all parts, laid end to end along the dimension named above; an argument that names none is the same for every part. Nothing has to cross between parts.
Inputs may be any that keep to these rules, and one draw needn't show every extreme that they name: `tactic_goal`: every goal is read by at least one tactic; tactics per goal are uneven. `tactic_len`: the live positions of a tactic are its leading ones.
All inputs are finite; a program needn't handle non-finite values.
Results may differ from the reference program's by a relative error of at most 0.01.
Values may be sent and summed in bfloat16 or wider, within the bound.
A program may use at most 192 MiB of HBM per device.

```python
import jax
import jax.numpy as jnp
from jax import lax

H = 64
DH = 64
D_OUT = 2048
LG = 256
LT = 64
GOALS = 16
TACTICS = 64


def draw_queries(key, part):
    base = 0.35 * jax.random.normal(jax.random.fold_in(key, 1), (TACTICS, LT, H * DH), jnp.float32)
    return jnp.clip(base, -8.0, 8.0).astype(jnp.bfloat16)


def draw_goal_keys(key, part):
    base = 0.35 * jax.random.normal(jax.random.fold_in(key, 2), (GOALS, LG, H * DH), jnp.float32)
    return jnp.clip(base, -8.0, 8.0).astype(jnp.bfloat16)


def touch_ends(values, rng, smallest, largest):
    longest = values.shape.index(max(values.shape))
    spots = []
    for shift in (0, 1):
        where = [jax.random.randint(jax.random.fold_in(rng, axis), (), 0, length) for axis, length in enumerate(values.shape)]
        where[longest] = (where[longest] + shift) % values.shape[longest]
        spots.append(tuple(where))
    return values.at[spots[0]].set(smallest).at[spots[1]].set(largest)


def shard_levels(rng, shape, shards, low, largest):
    level = 1.0
    for position, parts in shards:
        draws = jax.random.uniform(jax.random.fold_in(jax.random.fold_in(rng, 6), position), (parts,), jnp.float32, low / len(shards), largest / len(shards))
        level = level * jnp.repeat(jnp.exp(draws), shape[position] // parts).reshape((-1,) + (1,) * (len(shape) - 1 - position))
    return level


def different_ones(rng, rows, number_of, top, lift):
    ranking = jax.random.permutation(jax.random.fold_in(rng, 1), number_of)
    pull = ranking
    for power in range(3):
        pull = pull * pull // number_of
    pull = pull * lift // number_of
    tickets = jax.random.randint(jax.random.fold_in(rng, 2), (rows, number_of), 0, 4096) + pull
    sure = jax.random.permutation(jax.random.fold_in(rng, 3), rows)[jnp.arange(number_of) % rows]
    tickets = jnp.where(jnp.arange(rows)[:, None] == sure[None, :], 1 << 14, tickets)
    merit = tickets * number_of + jnp.arange(number_of)
    return lax.top_k(merit.astype(jnp.int32), top)[1].astype(jnp.int32)


def scatter_about(rng, extent, scale, most, split=(), kind=jnp.bfloat16):
    factor_of = shard_levels(rng, extent, split, -0.22, 0.18) if split else 1.0
    drawn = jax.random.normal(rng, extent, jnp.float32) * scale * factor_of
    return jnp.minimum(jnp.maximum(drawn, -most), most).astype(kind)


def setup_inputs(seed: int = 0, part: int = 0) -> dict:
    keys = jax.random.split(jax.random.key(seed), 7)
    own_keys = jax.random.split(jax.random.fold_in(keys[6], part), 7)
    return {
        "queries": draw_queries(jax.random.fold_in(jax.random.fold_in(keys[6], part), 71), part),
        "goal_keys": draw_goal_keys(jax.random.fold_in(jax.random.fold_in(keys[6], part), 71), part),
        "goal_values": scatter_about(own_keys[2], (GOALS, LG, H * DH), 1.0, 6.0, ((0, 16),)),
        "out_weight": scatter_about(keys[3], (H * DH, D_OUT), (H * DH // 32) ** -0.5, 0.5, ((0, 16),)),
        "tactic_goal": different_ones(own_keys[4], TACTICS, GOALS, 1, 1024),
        "tactic_len": touch_ends(jax.random.randint(own_keys[5], (TACTICS,), 1, LT + 1), jax.random.fold_in(own_keys[5], 1), 1, LT).astype(jnp.int32),
    }


def reference(queries, goal_keys, goal_values, out_weight, tactic_goal, tactic_len):
    goal_ids = tactic_goal[:, 0].astype(jnp.int32)

    def one_tactic(operands):
        query_rows, goal_index, live_count = operands
        keys_rows = lax.dynamic_index_in_dim(goal_keys, goal_index, 0, keepdims=False)
        value_rows = lax.dynamic_index_in_dim(goal_values, goal_index, 0, keepdims=False)
        query_four = query_rows.astype(jnp.float32).reshape(LT, H, DH)
        keys_four = keys_rows.astype(jnp.float32).reshape(LG, H, DH)
        value_four = value_rows.astype(jnp.float32).reshape(LG, H, DH)
        scores = jnp.einsum("ihd,jhd->hij", query_four, keys_four)
        biggest = jnp.max(scores, axis=-1, keepdims=True)
        powers = jnp.exp(scores - biggest)
        weights = (powers / jnp.sum(powers, axis=-1, keepdims=True)).astype(jnp.bfloat16)
        attended = jnp.einsum("hij,jhd->ihd", weights.astype(jnp.float32), value_four)
        attended = attended.reshape(LT, H * DH).astype(jnp.bfloat16)
        live_rows = jnp.arange(LT) < live_count
        return jnp.where(live_rows[:, None], attended, jnp.zeros_like(attended))

    context = lax.map(one_tactic, (queries, goal_ids, tactic_len))
    flat = context.reshape(TACTICS * LT, H * DH)
    projected = jnp.dot(flat, out_weight, preferred_element_type=jnp.float32).astype(jnp.bfloat16)
    return projected.reshape(TACTICS, LT, D_OUT)
```

```python
import functools

import jax
import jax.numpy as jnp
from jax import lax
from jax.experimental import pallas as pl
from jax.experimental.pallas import tpu as pltpu
from jax.sharding import PartitionSpec as P

DH = 64
LANES = 128
MESH = pl.DeviceIdType.MESH


def attend(query_piece, keys_heads, values_heads, goal_ids):
    row_count = query_piece.shape[1]
    width_local = query_piece.shape[2]
    head_count = width_local // DH

    def one_tactic(operands):
        query_rows, goal = operands
        keys = lax.dynamic_index_in_dim(keys_heads, goal, 0, keepdims=False).reshape(-1, head_count, DH)
        values = lax.dynamic_index_in_dim(values_heads, goal, 0, keepdims=False).reshape(-1, head_count, DH)
        query_three = query_rows.reshape(row_count, head_count, DH)
        scores = jnp.einsum("ihd,jhd->hij", query_three, keys, preferred_element_type=jnp.float32)
        powers = jnp.exp(scores - jnp.max(scores, axis=-1, keepdims=True))
        weights = (powers / jnp.sum(powers, axis=-1, keepdims=True)).astype(jnp.bfloat16)
        attended = jnp.einsum("hij,jhd->ihd", weights, values, preferred_element_type=jnp.float32)
        return attended.reshape(row_count, width_local).astype(jnp.bfloat16)

    return lax.map(one_tactic, (query_piece, goal_ids))


def plain_shards(queries, goal_keys, goal_values, out_weight, tactic_goal, tactic_len):
    goal_ids = lax.all_gather(tactic_goal[:, 0], "goal", axis=0, tiled=True)
    keys_heads, values_heads = (
        lax.all_to_all(goal_keys, "goal", split_axis=2, concat_axis=0, tiled=True),
        lax.all_to_all(goal_values, "goal", split_axis=2, concat_axis=0, tiled=True),
    )
    query_heads = lax.all_to_all(queries, "goal", split_axis=2, concat_axis=0, tiled=True)
    attended = attend(query_heads, keys_heads, values_heads, goal_ids)
    merged = lax.all_to_all(attended, "goal", split_axis=0, concat_axis=2, tiled=True)
    live_rows = jnp.arange(merged.shape[1])[None, :] < tactic_len[:, None]
    context = jnp.where(live_rows[:, :, None], merged, jnp.zeros_like(merged))
    tact_local = context.shape[0]
    row_count = context.shape[1]
    flat = context.reshape(tact_local * row_count, context.shape[2])
    projected = jnp.dot(
        flat,
        lax.all_gather(out_weight, "goal", axis=0, tiled=True),
        preferred_element_type=jnp.float32,
    )
    return projected.astype(jnp.bfloat16).reshape(tact_local, row_count, out_weight.shape[1])


def attend_kernel(n, chunks, ids_ref, q_hbm, k_hbm, v_hbm, ctx_hbm,
                  ids_all, ids_smem, qb, ob,
                  send_sem, recv_sem, ids_send, ids_recv, local_sem, *held):
    keys_at, values_at = held[:chunks], held[chunks:]
    me = lax.axis_index("goal")
    tacts = q_hbm.shape[0]
    rows = q_hbm.shape[1]
    width = chunks * LANES

    def peer_of(i):
        return lax.rem(me + lax.rem(i * 7, n), n)

    def columns(owner, c):
        return pl.ds(pl.multiple_of(owner * width + c * LANES, LANES), LANES)

    def source(kind, c, owner):
        if kind == 0:
            return q_hbm.at[:, :, columns(owner, c)]
        return (k_hbm if kind == 1 else v_hbm).at[0, :, columns(owner, c)]

    def landing(kind, c, slot):
        if kind == 0:
            return qb.at[c, slot]
        return (keys_at if kind == 1 else values_at)[c].at[slot]

    def in_copy(kind, c, peer, slot_at_dest, recv_slot):
        return pltpu.make_async_remote_copy(
            src_ref=source(kind, c, peer),
            dst_ref=landing(kind, c, slot_at_dest),
            send_sem=send_sem.at[c * 4 + kind, peer],
            recv_sem=recv_sem.at[c * 4 + kind, recv_slot],
            device_id={"goal": peer},
            device_id_type=MESH,
        )

    def out_copy(c, peer, slot_at_dest, recv_slot):
        return pltpu.make_async_remote_copy(
            src_ref=ob.at[c, peer],
            dst_ref=ctx_hbm.at[:, :, columns(slot_at_dest, c)],
            send_sem=send_sem.at[c * 4 + 3, peer],
            recv_sem=recv_sem.at[c * 4 + 3, recv_slot],
            device_id={"goal": peer},
            device_id_type=MESH,
        )

    def ids_copy(peer, slot_at_dest, recv_slot):
        return pltpu.make_async_remote_copy(
            src_ref=ids_ref,
            dst_ref=ids_all.at[slot_at_dest],
            send_sem=ids_send.at[peer],
            recv_sem=ids_recv.at[recv_slot],
            device_id={"goal": peer},
            device_id_type=MESH,
        )

    def each_peer(body):
        def step(i, carry):
            body(peer_of(i))
            return carry
        lax.fori_loop(1, n, step, 0)

    barrier = pltpu.get_barrier_semaphore()
    each_peer(lambda p: pl.semaphore_signal(barrier, inc=1, device_id={"goal": p}, device_id_type=MESH))
    pl.semaphore_wait(barrier, n - 1)

    each_peer(lambda p: ids_copy(p, me, me).start())
    for c in range(chunks):
        for kind in (1, 0, 2):
            each_peer(lambda p, kind=kind, c=c: in_copy(kind, c, p, me, me).start())

    ids_all[me] = ids_ref[...]
    own = []
    for c in range(chunks):
        for kind in range(3):
            own.append(pltpu.make_async_copy(source(kind, c, me), landing(kind, c, me), local_sem.at[c * 4 + kind]))
    for copy in own:
        copy.start()
    for copy in own:
        copy.wait()

    each_peer(lambda p: ids_copy(p, p, p).wait_recv())
    to_scalar = pltpu.make_async_copy(ids_all, ids_smem, local_sem.at[3])
    to_scalar.start()
    to_scalar.wait()

    lane = lax.broadcasted_iota(jnp.int32, (rows, LANES), 1)
    first = lane < DH

    for c in range(chunks):
        for kind in (1, 0, 2):
            each_peer(lambda p, kind=kind, c=c: in_copy(kind, c, p, p, p).wait_recv())

        def one_tactic(p, t, c=c):
            goal = ids_smem[p, 0, t]
            q = qb[c, p, t]
            zero = jnp.zeros_like(q)
            both = jnp.concatenate([jnp.where(first, q, zero), jnp.where(first, zero, q)], axis=0)
            k = keys_at[c][goal]
            v = values_at[c][goal]
            s = lax.dot_general(both, k, (((1,), (1,)), ((), ())), preferred_element_type=jnp.float32)
            e = jnp.exp(s - jnp.max(s, axis=-1, keepdims=True))
            total = jnp.sum(e, axis=-1, keepdims=True)
            o = jnp.dot(e.astype(jnp.bfloat16), v, preferred_element_type=jnp.float32)
            o = o * (1.0 / total)
            ob[c, p, t] = jnp.where(first, o[:rows], o[rows:]).astype(jnp.bfloat16)

        def one_peer(p, c=c):
            for t in range(tacts):
                one_tactic(p, t)

        def step(i, carry, c=c):
            p = peer_of(i)
            one_peer(p)
            out_copy(c, p, me, me).start()
            return carry

        lax.fori_loop(1, n, step, 0)
        one_peer(me)
        back = pltpu.make_async_copy(ob.at[c, me], ctx_hbm.at[:, :, columns(me, c)], local_sem.at[c * 4 + 3])
        back.start()
        back.wait()

    each_peer(lambda p: ids_copy(p, me, me).wait_send())
    for c in range(chunks):
        for kind in range(3):
            each_peer(lambda p, kind=kind, c=c: in_copy(kind, c, p, me, me).wait_send())
    for c in range(chunks):
        each_peer(lambda p, c=c: out_copy(c, p, me, me).wait_send())
        each_peer(lambda p, c=c: out_copy(c, p, p, p).wait_recv())


def attend_exchange(n, ids, queries, goal_keys, goal_values):
    tacts, rows, features = queries.shape
    tokens = goal_keys.shape[1]
    chunks = features // n // LANES
    anywhere = pl.BlockSpec(memory_space=pl.ANY)
    bf16 = jnp.bfloat16
    return pl.pallas_call(
        functools.partial(attend_kernel, n, chunks),
        out_shape=jax.ShapeDtypeStruct(queries.shape, bf16),
        in_specs=[pl.BlockSpec(memory_space=pltpu.VMEM), anywhere, anywhere, anywhere],
        out_specs=anywhere,
        scratch_shapes=[
            pltpu.VMEM((n, 8, LANES), jnp.int32),
            pltpu.SMEM((n, 8, LANES), jnp.int32),
            pltpu.VMEM((chunks, n, tacts, rows, LANES), bf16),
            pltpu.VMEM((chunks, n, tacts, rows, LANES), bf16),
            pltpu.SemaphoreType.DMA((chunks * 4, n)),
            pltpu.SemaphoreType.DMA((chunks * 4, n)),
            pltpu.SemaphoreType.DMA((n,)),
            pltpu.SemaphoreType.DMA((n,)),
            pltpu.SemaphoreType.DMA((chunks * 4,)),
        ]
        + [pltpu.VMEM((n, tokens, LANES), bf16)] * (2 * chunks),
        compiler_params=pltpu.CompilerParams(
            collective_id=0, has_side_effects=True, vmem_limit_bytes=32 * 1024 * 1024
        ),
        cost_estimate=pl.CostEstimate(
            flops=8 * tacts * n * rows * tokens * features // n,
            bytes_accessed=400 * 1024 * 1024,
            transcendentals=0,
        ),
    )(ids, queries, goal_keys, goal_values)


def direct_shards(n, queries, goal_keys, goal_values, out_weight, tactic_goal, tactic_len):
    tacts, rows, features = queries.shape
    ids = jnp.pad(tactic_goal.reshape(1, tacts), ((0, 7), (0, LANES - tacts)))
    weight = lax.all_gather(out_weight, "goal", axis=0, tiled=True)
    context = attend_exchange(n, ids, queries, goal_keys, goal_values)
    projected = jnp.dot(
        context.reshape(tacts * rows, features), weight, preferred_element_type=jnp.float32
    ).astype(jnp.bfloat16).reshape(tacts, rows, weight.shape[1])
    live_rows = jnp.arange(rows)[None, :] < tactic_len[:, None]
    return jnp.where(live_rows[:, :, None], projected, jnp.zeros_like(projected))


def solution(mesh):
    n = mesh.shape["goal"]

    def shards(queries, goal_keys, goal_values, out_weight, tactic_goal, tactic_len):
        fits = (
            n > 1 and n % 7 != 0
            and queries.shape[2] % (n * LANES) == 0
            and goal_keys.shape[0] == 1
            and queries.shape[0] <= LANES
        )
        body = functools.partial(direct_shards, n) if fits else plain_shards
        return body(queries, goal_keys, goal_values, out_weight, tactic_goal, tactic_len)

    return jax.shard_map(
        shards,
        mesh=mesh,
        in_specs=(
            P(("groups", "goal"), None, None),
            P(("groups", "goal"), None, None),
            P(("groups", "goal"), None, None),
            P("goal", None),
            P(("groups", "goal"), None),
            P(("groups", "goal")),
        ),
        out_specs=P(("groups", "goal"), None, None),
        check_vma=False,
    )
```

```python
import functools

import jax
import jax.numpy as jnp
from jax import lax
from jax.experimental import pallas as pl
from jax.experimental.pallas import tpu as pltpu
from jax.sharding import PartitionSpec as P

DH = 64
LANES = 128
MESH = pl.DeviceIdType.MESH


def attend(query_piece, keys_heads, values_heads, goal_ids):
    row_count = query_piece.shape[1]
    width_local = query_piece.shape[2]
    head_count = width_local // DH

    def one_tactic(operands):
        query_rows, goal = operands
        keys = lax.dynamic_index_in_dim(keys_heads, goal, 0, keepdims=False).reshape(-1, head_count, DH)
        values = lax.dynamic_index_in_dim(values_heads, goal, 0, keepdims=False).reshape(-1, head_count, DH)
        query_three = query_rows.reshape(row_count, head_count, DH)
        scores = jnp.einsum("ihd,jhd->hij", query_three, keys, preferred_element_type=jnp.float32)
        powers = jnp.exp(scores - jnp.max(scores, axis=-1, keepdims=True))
        weights = (powers / jnp.sum(powers, axis=-1, keepdims=True)).astype(jnp.bfloat16)
        attended = jnp.einsum("hij,jhd->ihd", weights, values, preferred_element_type=jnp.float32)
        return attended.reshape(row_count, width_local).astype(jnp.bfloat16)

    return lax.map(one_tactic, (query_piece, goal_ids))


def plain_shards(queries, goal_keys, goal_values, out_weight, tactic_goal, tactic_len):
    goal_ids = lax.all_gather(tactic_goal[:, 0], "goal", axis=0, tiled=True)
    keys_heads, values_heads = (
        lax.all_to_all(goal_keys, "goal", split_axis=2, concat_axis=0, tiled=True),
        lax.all_to_all(goal_values, "goal", split_axis=2, concat_axis=0, tiled=True),
    )
    query_heads = lax.all_to_all(queries, "goal", split_axis=2, concat_axis=0, tiled=True)
    attended = attend(query_heads, keys_heads, values_heads, goal_ids)
    merged = lax.all_to_all(attended, "goal", split_axis=0, concat_axis=2, tiled=True)
    live_rows = jnp.arange(merged.shape[1])[None, :] < tactic_len[:, None]
    context = jnp.where(live_rows[:, :, None], merged, jnp.zeros_like(merged))
    tact_local = context.shape[0]
    row_count = context.shape[1]
    flat = context.reshape(tact_local * row_count, context.shape[2])
    projected = jnp.dot(
        flat,
        lax.all_gather(out_weight, "goal", axis=0, tiled=True),
        preferred_element_type=jnp.float32,
    )
    return projected.astype(jnp.bfloat16).reshape(tact_local, row_count, out_weight.shape[1])


def attend_kernel(n, chunks, ids_ref, q_hbm, k_hbm, v_hbm, w_hbm, ctx_hbm, w_all,
                  ids_all, ids_smem, qb, ob,
                  send_sem, recv_sem, ids_send, ids_recv, local_sem, w_send, w_recv, w_local, *held):
    keys_at, values_at = held[:chunks], held[chunks:]
    me = lax.axis_index("goal")
    tacts = q_hbm.shape[0]
    rows = q_hbm.shape[1]
    width = chunks * LANES

    def peer_of(i):
        return lax.rem(me + lax.rem(i * 7, n), n)

    def columns(owner, c):
        return pl.ds(pl.multiple_of(owner * width + c * LANES, LANES), LANES)

    def source(kind, c, owner):
        if kind == 0:
            return q_hbm.at[:, :, columns(owner, c)]
        return (k_hbm if kind == 1 else v_hbm).at[0, :, columns(owner, c)]

    def landing(kind, c, slot):
        if kind == 0:
            return qb.at[c, slot]
        return (keys_at if kind == 1 else values_at)[c].at[slot]

    def in_copy(kind, c, peer, slot_at_dest, recv_slot):
        return pltpu.make_async_remote_copy(
            src_ref=source(kind, c, peer),
            dst_ref=landing(kind, c, slot_at_dest),
            send_sem=send_sem.at[c * 4 + kind, peer],
            recv_sem=recv_sem.at[c * 4 + kind, recv_slot],
            device_id={"goal": peer},
            device_id_type=MESH,
        )

    def out_copy(c, peer, slot_at_dest, recv_slot):
        return pltpu.make_async_remote_copy(
            src_ref=ob.at[c, peer],
            dst_ref=ctx_hbm.at[:, :, columns(slot_at_dest, c)],
            send_sem=send_sem.at[c * 4 + 3, peer],
            recv_sem=recv_sem.at[c * 4 + 3, recv_slot],
            device_id={"goal": peer},
            device_id_type=MESH,
        )

    def ids_copy(peer, slot_at_dest, recv_slot):
        return pltpu.make_async_remote_copy(
            src_ref=ids_ref,
            dst_ref=ids_all.at[slot_at_dest],
            send_sem=ids_send.at[peer],
            recv_sem=ids_recv.at[recv_slot],
            device_id={"goal": peer},
            device_id_type=MESH,
        )

    def each_peer(body):
        def step(i, carry):
            body(peer_of(i))
            return carry
        lax.fori_loop(1, n, step, 0)

    group = lax.axis_index("groups")
    half_rows = w_hbm.shape[0] // 2
    z, y, core = me // 4, lax.rem(me // 2, 2), lax.rem(me, 2)
    across = {"groups": 1 - group}
    up, down = {"goal": lax.rem(me + 4, n)}, {"goal": lax.rem(me + n - 4, n)}
    beside = {"goal": me + 2 - 4 * y}
    twin = {"goal": me + 1 - 2 * core}

    def half(ref, h):
        return ref.at[pl.ds(pl.multiple_of(h * half_rows, half_rows), half_rows)]

    def w_copy(slot, h, send, dest):
        return pltpu.make_async_remote_copy(
            src_ref=half(w_all.at[slot], h),
            dst_ref=half(w_all.at[slot], h),
            send_sem=w_send.at[send],
            recv_sem=w_recv.at[slot * 2 + h],
            device_id=dest,
            device_id_type=MESH,
        )

    def own_copy(h, send, dest):
        return pltpu.make_async_remote_copy(
            src_ref=half(w_hbm, h),
            dst_ref=half(w_all.at[me], h),
            send_sem=w_send.at[send],
            recv_sem=w_recv.at[me * 2 + h],
            device_id=dest,
            device_id_type=MESH,
        )

    def arrive(slot, h):
        w_copy(slot, h, 0, twin).wait_recv()

    w_own = pltpu.make_async_copy(w_hbm, w_all.at[me], w_local.at[0])
    sends = []

    def own_sends():
        w_own.start()
        for dest, send, when in ((up, 0, z < 3), (down, 1, z > 0)):
            copy = own_copy(group, send, dest)
            pl.when(when)(copy.start)
            sends.append((copy, when))
        copy = own_copy(group, 2, beside)
        copy.start()
        sends.append((copy, None))
        for h in range(2):
            copy = own_copy(h, 3 + h, twin)
            copy.start()
            sends.append((copy, None))

    def z_steps():
        for d in range(1, 4):
            for side in range(2):
                there = z - d if side == 0 else z + d
                held_here = there >= 0 if side == 0 else there <= 3
                slot = lax.rem(me + (n - 4 * d if side == 0 else 4 * d), n)
                base = 5 + (d * 2 + side - 2) * 4
                onward = held_here & (z < 3 if side == 0 else z > 0)
                copies = [
                    (w_copy(slot, group, base, up if side == 0 else down), onward),
                    (w_copy(slot, group, base + 1, beside), held_here),
                    (w_copy(slot, group, base + 2, across), held_here),
                    (w_copy(slot, group, base + 3, twin), held_here),
                ]
                pl.when(held_here)(functools.partial(arrive, slot, group))
                for copy, when in copies:
                    pl.when(when)(copy.start)
                    sends.append((copy, when))

    def y_steps():
        for d in range(4):
            slot = lax.rem(me + 2 - 4 * y + 4 * d + n, n)
            arrive(slot, group)
            for copy in (w_copy(slot, group, 29 + 2 * d, across), w_copy(slot, group, 30 + 2 * d, twin)):
                copy.start()
                sends.append((copy, None))

    def x_steps():
        for d in range(1, 8):
            slot = lax.rem(me + 2 * d, n)
            arrive(slot, 1 - group)
            copy = w_copy(slot, 1 - group, 36 + d, twin)
            copy.start()
            sends.append((copy, None))

    def twin_steps():
        for d in range(8):
            for h in range(2):
                arrive(lax.rem(me + 1 - 2 * core + 2 * d + n, n), h)
        for copy, when in sends:
            if when is None:
                copy.wait_send()
            else:
                pl.when(when)(copy.wait_send)
        w_own.wait()

    barrier = pltpu.get_barrier_semaphore()
    pl.semaphore_signal(barrier, inc=1, device_id=across, device_id_type=MESH)
    each_peer(lambda p: pl.semaphore_signal(barrier, inc=1, device_id={"goal": p}, device_id_type=MESH))
    pl.semaphore_wait(barrier, n)

    each_peer(lambda p: ids_copy(p, me, me).start())
    for c in range(chunks):
        for kind in (1, 0, 2):
            each_peer(lambda p, kind=kind, c=c: in_copy(kind, c, p, me, me).start())
        if c == 0:
            own_sends()

    ids_all[me] = ids_ref[...]
    own = []
    for c in range(chunks):
        for kind in range(3):
            own.append(pltpu.make_async_copy(source(kind, c, me), landing(kind, c, me), local_sem.at[c * 4 + kind]))
    for copy in own:
        copy.start()
    for copy in own:
        copy.wait()

    each_peer(lambda p: ids_copy(p, p, p).wait_recv())
    to_scalar = pltpu.make_async_copy(ids_all, ids_smem, local_sem.at[3])
    to_scalar.start()
    to_scalar.wait()

    z_steps()
    y_steps()

    lane = lax.broadcasted_iota(jnp.int32, (rows, LANES), 1)
    first = lane < DH

    for c in range(chunks):
        for kind in (1, 0, 2):
            each_peer(lambda p, kind=kind, c=c: in_copy(kind, c, p, p, p).wait_recv())

        def one_tactic(p, t, c=c):
            goal = ids_smem[p, 0, t]
            q = qb[c, p, t]
            zero = jnp.zeros_like(q)
            both = jnp.concatenate([jnp.where(first, q, zero), jnp.where(first, zero, q)], axis=0)
            k = keys_at[c][goal]
            v = values_at[c][goal]
            s = lax.dot_general(both, k, (((1,), (1,)), ((), ())), preferred_element_type=jnp.float32)
            e = jnp.exp(s - jnp.max(s, axis=-1, keepdims=True))
            total = jnp.sum(e, axis=-1, keepdims=True)
            o = jnp.dot(e.astype(jnp.bfloat16), v, preferred_element_type=jnp.float32)
            o = o * (1.0 / total)
            ob[c, p, t] = jnp.where(first, o[:rows], o[rows:]).astype(jnp.bfloat16)

        def one_peer(p, c=c):
            for t in range(tacts):
                one_tactic(p, t)

        def step(i, carry, c=c):
            p = peer_of(i)
            one_peer(p)
            out_copy(c, p, me, me).start()
            return carry

        lax.fori_loop(1, n, step, 0)
        one_peer(me)
        back = pltpu.make_async_copy(ob.at[c, me], ctx_hbm.at[:, :, columns(me, c)], local_sem.at[c * 4 + 3])
        back.start()
        back.wait()
        if c == 0:
            x_steps()

    twin_steps()
    each_peer(lambda p: ids_copy(p, me, me).wait_send())
    for c in range(chunks):
        for kind in range(3):
            each_peer(lambda p, kind=kind, c=c: in_copy(kind, c, p, me, me).wait_send())
    for c in range(chunks):
        each_peer(lambda p, c=c: out_copy(c, p, me, me).wait_send())
        each_peer(lambda p, c=c: out_copy(c, p, p, p).wait_recv())


def attend_exchange(n, ids, queries, goal_keys, goal_values, out_weight):
    tacts, rows, features = queries.shape
    tokens = goal_keys.shape[1]
    chunks = features // n // LANES
    anywhere = pl.BlockSpec(memory_space=pl.ANY)
    bf16 = jnp.bfloat16
    return pl.pallas_call(
        functools.partial(attend_kernel, n, chunks),
        out_shape=(
            jax.ShapeDtypeStruct(queries.shape, bf16),
            jax.ShapeDtypeStruct((n, *out_weight.shape), bf16),
        ),
        in_specs=[pl.BlockSpec(memory_space=pltpu.VMEM)] + [anywhere] * 4,
        out_specs=(anywhere, anywhere),
        scratch_shapes=[
            pltpu.VMEM((n, 8, LANES), jnp.int32),
            pltpu.SMEM((n, 8, LANES), jnp.int32),
            pltpu.VMEM((chunks, n, tacts, rows, LANES), bf16),
            pltpu.VMEM((chunks, n, tacts, rows, LANES), bf16),
            pltpu.SemaphoreType.DMA((chunks * 4, n)),
            pltpu.SemaphoreType.DMA((chunks * 4, n)),
            pltpu.SemaphoreType.DMA((n,)),
            pltpu.SemaphoreType.DMA((n,)),
            pltpu.SemaphoreType.DMA((chunks * 4,)),
            pltpu.SemaphoreType.DMA((44,)),
            pltpu.SemaphoreType.DMA((2 * n,)),
            pltpu.SemaphoreType.DMA((1,)),
        ]
        + [pltpu.VMEM((n, tokens, LANES), bf16)] * (2 * chunks),
        compiler_params=pltpu.CompilerParams(
            collective_id=0, has_side_effects=True, vmem_limit_bytes=32 * 1024 * 1024
        ),
        cost_estimate=pl.CostEstimate(
            flops=8 * tacts * n * rows * tokens * features // n,
            bytes_accessed=400 * 1024 * 1024,
            transcendentals=0,
        ),
    )(ids, queries, goal_keys, goal_values, out_weight)


def direct_shards(n, queries, goal_keys, goal_values, out_weight, tactic_goal, tactic_len):
    tacts, rows, features = queries.shape
    ids = jnp.pad(tactic_goal.reshape(1, tacts), ((0, 7), (0, LANES - tacts)))
    context, weight = attend_exchange(n, ids, queries, goal_keys, goal_values, out_weight)
    weight = weight.reshape(features, out_weight.shape[1])
    projected = jnp.dot(
        context.reshape(tacts * rows, features), weight, preferred_element_type=jnp.float32
    ).astype(jnp.bfloat16).reshape(tacts, rows, weight.shape[1])
    live_rows = jnp.arange(rows)[None, :] < tactic_len[:, None]
    return jnp.where(live_rows[:, :, None], projected, jnp.zeros_like(projected))


def solution(mesh):
    n = mesh.shape["goal"]

    def shards(queries, goal_keys, goal_values, out_weight, tactic_goal, tactic_len):
        fits = (
            n == 16 and mesh.shape["groups"] == 2
            and out_weight.shape[0] % 32 == 0
            and queries.shape[2] % (n * LANES) == 0
            and goal_keys.shape[0] == 1
            and queries.shape[0] <= LANES
        )
        body = functools.partial(direct_shards, n) if fits else plain_shards
        return body(queries, goal_keys, goal_values, out_weight, tactic_goal, tactic_len)

    return jax.shard_map(
        shards,
        mesh=mesh,
        in_specs=(
            P(("groups", "goal"), None, None),
            P(("groups", "goal"), None, None),
            P(("groups", "goal"), None, None),
            P("goal", None),
            P(("groups", "goal"), None),
            P(("groups", "goal")),
        ),
        out_specs=P(("groups", "goal"), None, None),
        check_vma=False,
    )
```

```python
import functools

import jax
import jax.numpy as jnp
from jax import lax
from jax.experimental import pallas as pl
from jax.experimental.pallas import tpu as pltpu
from jax.sharding import PartitionSpec as P

DH = 64
LANES = 128
MESH = pl.DeviceIdType.MESH


def attend(query_piece, keys_heads, values_heads, goal_ids):
    row_count = query_piece.shape[1]
    width_local = query_piece.shape[2]
    head_count = width_local // DH

    def one_tactic(operands):
        query_rows, goal = operands
        keys = lax.dynamic_index_in_dim(keys_heads, goal, 0, keepdims=False).reshape(-1, head_count, DH)
        values = lax.dynamic_index_in_dim(values_heads, goal, 0, keepdims=False).reshape(-1, head_count, DH)
        query_three = query_rows.reshape(row_count, head_count, DH)
        scores = jnp.einsum("ihd,jhd->hij", query_three, keys, preferred_element_type=jnp.float32)
        powers = jnp.exp(scores - jnp.max(scores, axis=-1, keepdims=True))
        weights = (powers / jnp.sum(powers, axis=-1, keepdims=True)).astype(jnp.bfloat16)
        attended = jnp.einsum("hij,jhd->ihd", weights, values, preferred_element_type=jnp.float32)
        return attended.reshape(row_count, width_local).astype(jnp.bfloat16)

    return lax.map(one_tactic, (query_piece, goal_ids))


def plain_shards(queries, goal_keys, goal_values, out_weight, tactic_goal, tactic_len):
    goal_ids = lax.all_gather(tactic_goal[:, 0], "goal", axis=0, tiled=True)
    keys_heads, values_heads = (
        lax.all_to_all(goal_keys, "goal", split_axis=2, concat_axis=0, tiled=True),
        lax.all_to_all(goal_values, "goal", split_axis=2, concat_axis=0, tiled=True),
    )
    query_heads = lax.all_to_all(queries, "goal", split_axis=2, concat_axis=0, tiled=True)
    attended = attend(query_heads, keys_heads, values_heads, goal_ids)
    merged = lax.all_to_all(attended, "goal", split_axis=0, concat_axis=2, tiled=True)
    live_rows = jnp.arange(merged.shape[1])[None, :] < tactic_len[:, None]
    context = jnp.where(live_rows[:, :, None], merged, jnp.zeros_like(merged))
    tact_local = context.shape[0]
    row_count = context.shape[1]
    flat = context.reshape(tact_local * row_count, context.shape[2])
    projected = jnp.dot(
        flat,
        lax.all_gather(out_weight, "goal", axis=0, tiled=True),
        preferred_element_type=jnp.float32,
    )
    return projected.astype(jnp.bfloat16).reshape(tact_local, row_count, out_weight.shape[1])


def attend_kernel(n, chunks, ids_ref, q_hbm, k_hbm, v_hbm, w_hbm, ctx_hbm, w_all,
                  ids_all, ids_smem, qb, ob,
                  send_sem, recv_sem, ids_send, ids_recv, local_sem, w_send, w_recv, w_local, *held):
    keys_at, values_at = held[:chunks], held[chunks:]
    me = lax.axis_index("goal")
    tacts = q_hbm.shape[0]
    rows = q_hbm.shape[1]
    width = chunks * LANES

    def peer_of(i):
        return lax.rem(me + lax.rem(i * 7, n), n)

    def columns(owner, c):
        return pl.ds(pl.multiple_of(owner * width + c * LANES, LANES), LANES)

    def source(kind, c, owner):
        if kind == 0:
            return q_hbm.at[:, :, columns(owner, c)]
        return (k_hbm if kind == 1 else v_hbm).at[0, :, columns(owner, c)]

    def landing(kind, c, slot):
        if kind == 0:
            return qb.at[c, slot]
        return (keys_at if kind == 1 else values_at)[c].at[slot]

    def in_copy(kind, c, peer, slot_at_dest, recv_slot):
        return pltpu.make_async_remote_copy(
            src_ref=source(kind, c, peer),
            dst_ref=landing(kind, c, slot_at_dest),
            send_sem=send_sem.at[c * 4 + kind, peer],
            recv_sem=recv_sem.at[c * 4 + kind, recv_slot],
            device_id={"goal": peer},
            device_id_type=MESH,
        )

    def out_copy(c, peer, slot_at_dest, recv_slot):
        return pltpu.make_async_remote_copy(
            src_ref=ob.at[c, peer],
            dst_ref=ctx_hbm.at[:, :, columns(slot_at_dest, c)],
            send_sem=send_sem.at[c * 4 + 3, peer],
            recv_sem=recv_sem.at[c * 4 + 3, recv_slot],
            device_id={"goal": peer},
            device_id_type=MESH,
        )

    def ids_copy(peer, slot_at_dest, recv_slot):
        return pltpu.make_async_remote_copy(
            src_ref=ids_ref,
            dst_ref=ids_all.at[slot_at_dest],
            send_sem=ids_send.at[peer],
            recv_sem=ids_recv.at[recv_slot],
            device_id={"goal": peer},
            device_id_type=MESH,
        )

    def each_peer(body):
        def step(i, carry):
            body(peer_of(i))
            return carry
        lax.fori_loop(1, n, step, 0)

    group = lax.axis_index("groups")
    half_rows = w_hbm.shape[0] // 2
    z, y, core = me // 4, lax.rem(me // 2, 2), lax.rem(me, 2)
    across = {"groups": 1 - group}
    up, down = {"goal": lax.rem(me + 4, n)}, {"goal": lax.rem(me + n - 4, n)}
    beside = {"goal": me + 2 - 4 * y}
    twin = {"goal": me + 1 - 2 * core}

    def half(ref, h):
        return ref.at[pl.ds(pl.multiple_of(h * half_rows, half_rows), half_rows)]

    def w_copy(slot, h, send, dest):
        return pltpu.make_async_remote_copy(
            src_ref=half(w_all.at[slot], h),
            dst_ref=half(w_all.at[slot], h),
            send_sem=w_send.at[send],
            recv_sem=w_recv.at[slot * 2 + h],
            device_id=dest,
            device_id_type=MESH,
        )

    def own_copy(h, send, dest):
        return pltpu.make_async_remote_copy(
            src_ref=half(w_hbm, h),
            dst_ref=half(w_all.at[me], h),
            send_sem=w_send.at[send],
            recv_sem=w_recv.at[me * 2 + h],
            device_id=dest,
            device_id_type=MESH,
        )

    def arrive(slot, h):
        w_copy(slot, h, 0, twin).wait_recv()

    w_own = pltpu.make_async_copy(w_hbm, w_all.at[me], w_local.at[0])
    sends = []

    def own_sends():
        w_own.start()
        for dest, send, when in ((up, 0, z < 3), (down, 1, z > 0)):
            copy = own_copy(group, send, dest)
            pl.when(when)(copy.start)
            sends.append((copy, when))
        copy = own_copy(group, 2, beside)
        copy.start()
        sends.append((copy, None))
        for h in range(2):
            copy = own_copy(h, 3 + h, twin)
            copy.start()
            sends.append((copy, None))

    def z_steps(distances):
        for d in distances:
            for side in range(2):
                there = z - d if side == 0 else z + d
                held_here = there >= 0 if side == 0 else there <= 3
                slot = lax.rem(me + (n - 4 * d if side == 0 else 4 * d), n)
                base = 5 + (d * 2 + side - 2) * 4
                onward = held_here & (z < 3 if side == 0 else z > 0)
                copies = [
                    (w_copy(slot, group, base, up if side == 0 else down), onward),
                    (w_copy(slot, group, base + 1, beside), held_here),
                    (w_copy(slot, group, base + 2, across), held_here),
                    (w_copy(slot, group, base + 3, twin), held_here),
                ]
                pl.when(held_here)(functools.partial(arrive, slot, group))
                for copy, when in copies:
                    pl.when(when)(copy.start)
                    sends.append((copy, when))

    def y_steps():
        for d in range(4):
            slot = lax.rem(me + 2 - 4 * y + 4 * d + n, n)
            arrive(slot, group)
            for copy in (w_copy(slot, group, 29 + 2 * d, across), w_copy(slot, group, 30 + 2 * d, twin)):
                copy.start()
                sends.append((copy, None))

    def x_steps():
        for d in range(1, 8):
            slot = lax.rem(me + 2 * d, n)
            arrive(slot, 1 - group)
            copy = w_copy(slot, 1 - group, 36 + d, twin)
            copy.start()
            sends.append((copy, None))

    def twin_steps():
        for d in range(8):
            for h in range(2):
                arrive(lax.rem(me + 1 - 2 * core + 2 * d + n, n), h)
        for copy, when in sends:
            if when is None:
                copy.wait_send()
            else:
                pl.when(when)(copy.wait_send)
        w_own.wait()

    barrier = pltpu.get_barrier_semaphore()
    pl.semaphore_signal(barrier, inc=1, device_id=across, device_id_type=MESH)
    each_peer(lambda p: pl.semaphore_signal(barrier, inc=1, device_id={"goal": p}, device_id_type=MESH))
    pl.semaphore_wait(barrier, n)

    batches = [(c, kind) for c in range(chunks) for kind in (1, 0, 2)]

    def issue(count):
        for _ in range(min(count, len(batches))):
            c, kind = batches.pop(0)
            each_peer(lambda p: in_copy(kind, c, p, me, me).start())

    own_sends()
    each_peer(lambda p: ids_copy(p, me, me).start())
    issue(2)

    ids_all[me] = ids_ref[...]
    own = []
    for c in range(chunks):
        for kind in range(3):
            own.append(pltpu.make_async_copy(source(kind, c, me), landing(kind, c, me), local_sem.at[c * 4 + kind]))
    for copy in own:
        copy.start()
    for copy in own:
        copy.wait()

    each_peer(lambda p: ids_copy(p, p, p).wait_recv())
    to_scalar = pltpu.make_async_copy(ids_all, ids_smem, local_sem.at[3])
    to_scalar.start()
    to_scalar.wait()

    z_steps((1,))
    issue(1)
    z_steps((2,))
    issue(1)
    z_steps((3,))
    issue(1)
    y_steps()
    issue(len(batches))

    lane = lax.broadcasted_iota(jnp.int32, (rows, LANES), 1)
    first = lane < DH

    for c in range(chunks):
        for kind in (1, 0, 2):
            each_peer(lambda p, kind=kind, c=c: in_copy(kind, c, p, p, p).wait_recv())

        def one_tactic(p, t, c=c):
            goal = ids_smem[p, 0, t]
            q = qb[c, p, t]
            zero = jnp.zeros_like(q)
            both = jnp.concatenate([jnp.where(first, q, zero), jnp.where(first, zero, q)], axis=0)
            k = keys_at[c][goal]
            v = values_at[c][goal]
            s = lax.dot_general(both, k, (((1,), (1,)), ((), ())), preferred_element_type=jnp.float32)
            e = jnp.exp(s - jnp.max(s, axis=-1, keepdims=True))
            total = jnp.sum(e, axis=-1, keepdims=True)
            o = jnp.dot(e.astype(jnp.bfloat16), v, preferred_element_type=jnp.float32)
            o = o * (1.0 / total)
            ob[c, p, t] = jnp.where(first, o[:rows], o[rows:]).astype(jnp.bfloat16)

        def one_peer(p, c=c):
            for t in range(tacts):
                one_tactic(p, t)

        def step(i, carry, c=c):
            p = peer_of(i)
            one_peer(p)
            out_copy(c, p, me, me).start()
            return carry

        lax.fori_loop(1, n, step, 0)
        one_peer(me)
        back = pltpu.make_async_copy(ob.at[c, me], ctx_hbm.at[:, :, columns(me, c)], local_sem.at[c * 4 + 3])
        back.start()
        back.wait()
        if c == 0:
            x_steps()

    twin_steps()
    each_peer(lambda p: ids_copy(p, me, me).wait_send())
    for c in range(chunks):
        for kind in range(3):
            each_peer(lambda p, kind=kind, c=c: in_copy(kind, c, p, me, me).wait_send())
    for c in range(chunks):
        each_peer(lambda p, c=c: out_copy(c, p, me, me).wait_send())
        each_peer(lambda p, c=c: out_copy(c, p, p, p).wait_recv())


def attend_exchange(n, ids, queries, goal_keys, goal_values, out_weight):
    tacts, rows, features = queries.shape
    tokens = goal_keys.shape[1]
    chunks = features // n // LANES
    anywhere = pl.BlockSpec(memory_space=pl.ANY)
    bf16 = jnp.bfloat16
    return pl.pallas_call(
        functools.partial(attend_kernel, n, chunks),
        out_shape=(
            jax.ShapeDtypeStruct(queries.shape, bf16),
            jax.ShapeDtypeStruct((n, *out_weight.shape), bf16),
        ),
        in_specs=[pl.BlockSpec(memory_space=pltpu.VMEM)] + [anywhere] * 4,
        out_specs=(anywhere, anywhere),
        scratch_shapes=[
            pltpu.VMEM((n, 8, LANES), jnp.int32),
            pltpu.SMEM((n, 8, LANES), jnp.int32),
            pltpu.VMEM((chunks, n, tacts, rows, LANES), bf16),
            pltpu.VMEM((chunks, n, tacts, rows, LANES), bf16),
            pltpu.SemaphoreType.DMA((chunks * 4, n)),
            pltpu.SemaphoreType.DMA((chunks * 4, n)),
            pltpu.SemaphoreType.DMA((n,)),
            pltpu.SemaphoreType.DMA((n,)),
            pltpu.SemaphoreType.DMA((chunks * 4,)),
            pltpu.SemaphoreType.DMA((44,)),
            pltpu.SemaphoreType.DMA((2 * n,)),
            pltpu.SemaphoreType.DMA((1,)),
        ]
        + [pltpu.VMEM((n, tokens, LANES), bf16)] * (2 * chunks),
        compiler_params=pltpu.CompilerParams(
            collective_id=0, has_side_effects=True, vmem_limit_bytes=60 * 1024 * 1024
        ),
        cost_estimate=pl.CostEstimate(
            flops=8 * tacts * n * rows * tokens * features // n,
            bytes_accessed=400 * 1024 * 1024,
            transcendentals=0,
        ),
    )(ids, queries, goal_keys, goal_values, out_weight)


def direct_shards(n, queries, goal_keys, goal_values, out_weight, tactic_goal, tactic_len):
    tacts, rows, features = queries.shape
    ids = jnp.pad(tactic_goal.reshape(1, tacts), ((0, 7), (0, LANES - tacts)))
    context, weight = attend_exchange(n, ids, queries, goal_keys, goal_values, out_weight)
    weight = weight.reshape(features, out_weight.shape[1])
    projected = jnp.dot(
        context.reshape(tacts * rows, features), weight, preferred_element_type=jnp.float32
    ).astype(jnp.bfloat16).reshape(tacts, rows, weight.shape[1])
    live_rows = jnp.arange(rows)[None, :] < tactic_len[:, None]
    return jnp.where(live_rows[:, :, None], projected, jnp.zeros_like(projected))


def solution(mesh):
    n = mesh.shape["goal"]

    def shards(queries, goal_keys, goal_values, out_weight, tactic_goal, tactic_len):
        fits = (
            n == 16 and mesh.shape["groups"] == 2
            and out_weight.shape[0] % 32 == 0
            and queries.shape[2] % (n * LANES) == 0
            and goal_keys.shape[0] == 1
            and queries.shape[0] <= LANES
        )
        body = functools.partial(direct_shards, n) if fits else plain_shards
        return body(queries, goal_keys, goal_values, out_weight, tactic_goal, tactic_len)

    return jax.shard_map(
        shards,
        mesh=mesh,
        in_specs=(
            P(("groups", "goal"), None, None),
            P(("groups", "goal"), None, None),
            P(("groups", "goal"), None, None),
            P("goal", None),
            P(("groups", "goal"), None),
            P(("groups", "goal")),
        ),
        out_specs=P(("groups", "goal"), None, None),
        check_vma=False,
    )
```

```python
import functools

import jax
import jax.numpy as jnp
from jax import lax
from jax.experimental import pallas as pl
from jax.experimental.pallas import tpu as pltpu
from jax.sharding import PartitionSpec as P

DH = 64
LANES = 128
MESH = pl.DeviceIdType.MESH


def attend(query_piece, keys_heads, values_heads, goal_ids):
    row_count = query_piece.shape[1]
    width_local = query_piece.shape[2]
    head_count = width_local // DH

    def one_tactic(operands):
        query_rows, goal = operands
        keys = lax.dynamic_index_in_dim(keys_heads, goal, 0, keepdims=False).reshape(-1, head_count, DH)
        values = lax.dynamic_index_in_dim(values_heads, goal, 0, keepdims=False).reshape(-1, head_count, DH)
        query_three = query_rows.reshape(row_count, head_count, DH)
        scores = jnp.einsum("ihd,jhd->hij", query_three, keys, preferred_element_type=jnp.float32)
        powers = jnp.exp(scores - jnp.max(scores, axis=-1, keepdims=True))
        weights = (powers / jnp.sum(powers, axis=-1, keepdims=True)).astype(jnp.bfloat16)
        attended = jnp.einsum("hij,jhd->ihd", weights, values, preferred_element_type=jnp.float32)
        return attended.reshape(row_count, width_local).astype(jnp.bfloat16)

    return lax.map(one_tactic, (query_piece, goal_ids))


def plain_shards(queries, goal_keys, goal_values, out_weight, tactic_goal, tactic_len):
    goal_ids = lax.all_gather(tactic_goal[:, 0], "goal", axis=0, tiled=True)
    keys_heads, values_heads = (
        lax.all_to_all(goal_keys, "goal", split_axis=2, concat_axis=0, tiled=True),
        lax.all_to_all(goal_values, "goal", split_axis=2, concat_axis=0, tiled=True),
    )
    query_heads = lax.all_to_all(queries, "goal", split_axis=2, concat_axis=0, tiled=True)
    attended = attend(query_heads, keys_heads, values_heads, goal_ids)
    merged = lax.all_to_all(attended, "goal", split_axis=0, concat_axis=2, tiled=True)
    live_rows = jnp.arange(merged.shape[1])[None, :] < tactic_len[:, None]
    context = jnp.where(live_rows[:, :, None], merged, jnp.zeros_like(merged))
    tact_local = context.shape[0]
    row_count = context.shape[1]
    flat = context.reshape(tact_local * row_count, context.shape[2])
    projected = jnp.dot(
        flat,
        lax.all_gather(out_weight, "goal", axis=0, tiled=True),
        preferred_element_type=jnp.float32,
    )
    return projected.astype(jnp.bfloat16).reshape(tact_local, row_count, out_weight.shape[1])


def attend_kernel(n, chunks, ids_ref, q_hbm, k_hbm, v_hbm, w_hbm, ctx_hbm, w_all,
                  ids_all, ids_smem, qb, ob,
                  send_sem, recv_sem, ids_send, ids_recv, local_sem, w_send, w_recv, w_local, *held):
    keys_at, values_at = held[:chunks], held[chunks:]
    me = lax.axis_index("goal")
    tacts = q_hbm.shape[0]
    rows = q_hbm.shape[1]
    width = chunks * LANES

    def peer_of(i):
        return lax.rem(me + i, n)

    def columns(owner, c):
        return pl.ds(pl.multiple_of(owner * width + c * LANES, LANES), LANES)

    def source(kind, c, owner):
        if kind == 0:
            return q_hbm.at[:, :, columns(owner, c)]
        return (k_hbm if kind == 1 else v_hbm).at[0, :, columns(owner, c)]

    def landing(kind, c, slot):
        if kind == 0:
            return qb.at[c, slot]
        return (keys_at if kind == 1 else values_at)[c].at[slot]

    def in_copy(kind, c, peer, slot_at_dest, recv_slot):
        return pltpu.make_async_remote_copy(
            src_ref=source(kind, c, peer),
            dst_ref=landing(kind, c, slot_at_dest),
            send_sem=send_sem.at[c * 4 + kind, peer],
            recv_sem=recv_sem.at[c * 4 + kind, recv_slot],
            device_id={"goal": peer},
            device_id_type=MESH,
        )

    def out_copy(c, peer, slot_at_dest, recv_slot):
        return pltpu.make_async_remote_copy(
            src_ref=ob.at[c, peer],
            dst_ref=ctx_hbm.at[:, :, columns(slot_at_dest, c)],
            send_sem=send_sem.at[c * 4 + 3, peer],
            recv_sem=recv_sem.at[c * 4 + 3, recv_slot],
            device_id={"goal": peer},
            device_id_type=MESH,
        )

    def ids_copy(peer, slot_at_dest, recv_slot):
        return pltpu.make_async_remote_copy(
            src_ref=ids_ref,
            dst_ref=ids_all.at[slot_at_dest],
            send_sem=ids_send.at[peer],
            recv_sem=ids_recv.at[recv_slot],
            device_id={"goal": peer},
            device_id_type=MESH,
        )

    def each_peer(body):
        def step(i, carry):
            body(peer_of(i))
            return carry
        lax.fori_loop(1, n, step, 0)

    group = lax.axis_index("groups")
    half_rows = w_hbm.shape[0] // 2
    z, y, core = me // 4, lax.rem(me // 2, 2), lax.rem(me, 2)
    across = {"groups": 1 - group}
    up, down = {"goal": lax.rem(me + 4, n)}, {"goal": lax.rem(me + n - 4, n)}
    beside = {"goal": me + 2 - 4 * y}
    twin = {"goal": me + 1 - 2 * core}

    def half(ref, h):
        return ref.at[pl.ds(pl.multiple_of(h * half_rows, half_rows), half_rows)]

    def w_copy(slot, h, send, dest):
        return pltpu.make_async_remote_copy(
            src_ref=half(w_all.at[slot], h),
            dst_ref=half(w_all.at[slot], h),
            send_sem=w_send.at[send],
            recv_sem=w_recv.at[slot * 2 + h],
            device_id=dest,
            device_id_type=MESH,
        )

    def own_copy(h, send, dest):
        return pltpu.make_async_remote_copy(
            src_ref=half(w_hbm, h),
            dst_ref=half(w_all.at[me], h),
            send_sem=w_send.at[send],
            recv_sem=w_recv.at[me * 2 + h],
            device_id=dest,
            device_id_type=MESH,
        )

    def arrive(slot, h):
        w_copy(slot, h, 0, twin).wait_recv()

    w_own = pltpu.make_async_copy(w_hbm, w_all.at[me], w_local.at[0])
    sends = []

    def own_sends():
        w_own.start()
        for dest, send, when in ((up, 0, z < 3), (down, 1, z > 0)):
            copy = own_copy(group, send, dest)
            pl.when(when)(copy.start)
            sends.append((copy, when))
        copy = own_copy(group, 2, beside)
        copy.start()
        sends.append((copy, None))
        for h in range(2):
            copy = own_copy(h, 3 + h, twin)
            copy.start()
            sends.append((copy, None))

    def z_steps(distances):
        for d in distances:
            for side in range(2):
                there = z - d if side == 0 else z + d
                held_here = there >= 0 if side == 0 else there <= 3
                slot = lax.rem(me + (n - 4 * d if side == 0 else 4 * d), n)
                base = 5 + (d * 2 + side - 2) * 4
                onward = held_here & (z < 3 if side == 0 else z > 0)
                copies = [
                    (w_copy(slot, group, base, up if side == 0 else down), onward),
                    (w_copy(slot, group, base + 1, beside), held_here),
                    (w_copy(slot, group, base + 2, across), held_here),
                    (w_copy(slot, group, base + 3, twin), held_here),
                ]
                pl.when(held_here)(functools.partial(arrive, slot, group))
                for copy, when in copies:
                    pl.when(when)(copy.start)
                    sends.append((copy, when))

    def y_steps():
        for d in range(4):
            slot = lax.rem(me + 2 - 4 * y + 4 * d + n, n)
            arrive(slot, group)
            for copy in (w_copy(slot, group, 29 + 2 * d, across), w_copy(slot, group, 30 + 2 * d, twin)):
                copy.start()
                sends.append((copy, None))

    def x_steps():
        for d in range(1, 8):
            slot = lax.rem(me + 2 * d, n)
            arrive(slot, 1 - group)
            copy = w_copy(slot, 1 - group, 36 + d, twin)
            copy.start()
            sends.append((copy, None))

    def twin_steps():
        for d in range(8):
            for h in range(2):
                arrive(lax.rem(me + 1 - 2 * core + 2 * d + n, n), h)
        for copy, when in sends:
            if when is None:
                copy.wait_send()
            else:
                pl.when(when)(copy.wait_send)
        w_own.wait()

    barrier = pltpu.get_barrier_semaphore()
    pl.semaphore_signal(barrier, inc=1, device_id=across, device_id_type=MESH)
    each_peer(lambda p: pl.semaphore_signal(barrier, inc=1, device_id={"goal": p}, device_id_type=MESH))
    pl.semaphore_wait(barrier, n)

    batches = [(c, kind) for c in range(chunks) for kind in (1, 0, 2)]

    def issue(count):
        for _ in range(min(count, len(batches))):
            c, kind = batches.pop(0)
            each_peer(lambda p: in_copy(kind, c, p, me, me).start())

    own_sends()
    each_peer(lambda p: ids_copy(p, me, me).start())
    issue(2)

    ids_all[me] = ids_ref[...]
    own = []
    for c in range(chunks):
        for kind in range(3):
            own.append(pltpu.make_async_copy(source(kind, c, me), landing(kind, c, me), local_sem.at[c * 4 + kind]))
    for copy in own:
        copy.start()
    z_steps((1,))
    issue(1)
    z_steps((2,))
    issue(1)
    z_steps((3,))
    issue(1)
    y_steps()
    issue(len(batches))

    for copy in own:
        copy.wait()

    each_peer(lambda p: ids_copy(p, p, p).wait_recv())
    to_scalar = pltpu.make_async_copy(ids_all, ids_smem, local_sem.at[3])
    to_scalar.start()
    to_scalar.wait()

    lane = lax.broadcasted_iota(jnp.int32, (rows, LANES), 1)
    first = lane < DH

    for c in range(chunks):
        for kind in (1, 0, 2):
            each_peer(lambda p, kind=kind, c=c: in_copy(kind, c, p, p, p).wait_recv())

        def one_tactic(p, t, c=c):
            goal = ids_smem[p, 0, t]
            q = qb[c, p, t]
            zero = jnp.zeros_like(q)
            both = jnp.concatenate([jnp.where(first, q, zero), jnp.where(first, zero, q)], axis=0)
            k = keys_at[c][goal]
            v = values_at[c][goal]
            s = lax.dot_general(both, k, (((1,), (1,)), ((), ())), preferred_element_type=jnp.float32)
            e = jnp.exp(s - jnp.max(s, axis=-1, keepdims=True))
            total = jnp.sum(e, axis=-1, keepdims=True)
            o = jnp.dot(e.astype(jnp.bfloat16), v, preferred_element_type=jnp.float32)
            o = o * (1.0 / total)
            ob[c, p, t] = jnp.where(first, o[:rows], o[rows:]).astype(jnp.bfloat16)

        def one_peer(p, c=c):
            for t in range(tacts):
                one_tactic(p, t)

        def step(i, carry, c=c):
            p = peer_of(i)
            one_peer(p)
            out_copy(c, p, me, me).start()
            return carry

        lax.fori_loop(1, n, step, 0)
        one_peer(me)
        back = pltpu.make_async_copy(ob.at[c, me], ctx_hbm.at[:, :, columns(me, c)], local_sem.at[c * 4 + 3])
        back.start()
        back.wait()
        if c == 0:
            x_steps()

    twin_steps()
    each_peer(lambda p: ids_copy(p, me, me).wait_send())
    for c in range(chunks):
        for kind in range(3):
            each_peer(lambda p, kind=kind, c=c: in_copy(kind, c, p, me, me).wait_send())
    for c in range(chunks):
        each_peer(lambda p, c=c: out_copy(c, p, me, me).wait_send())
        each_peer(lambda p, c=c: out_copy(c, p, p, p).wait_recv())


def attend_exchange(n, ids, queries, goal_keys, goal_values, out_weight):
    tacts, rows, features = queries.shape
    tokens = goal_keys.shape[1]
    chunks = features // n // LANES
    anywhere = pl.BlockSpec(memory_space=pl.ANY)
    bf16 = jnp.bfloat16
    return pl.pallas_call(
        functools.partial(attend_kernel, n, chunks),
        out_shape=(
            jax.ShapeDtypeStruct(queries.shape, bf16),
            jax.ShapeDtypeStruct((n, *out_weight.shape), bf16),
        ),
        in_specs=[pl.BlockSpec(memory_space=pltpu.VMEM)] + [anywhere] * 4,
        out_specs=(anywhere, anywhere),
        scratch_shapes=[
            pltpu.VMEM((n, 8, LANES), jnp.int32),
            pltpu.SMEM((n, 8, LANES), jnp.int32),
            pltpu.VMEM((chunks, n, tacts, rows, LANES), bf16),
            pltpu.VMEM((chunks, n, tacts, rows, LANES), bf16),
            pltpu.SemaphoreType.DMA((chunks * 4, n)),
            pltpu.SemaphoreType.DMA((chunks * 4, n)),
            pltpu.SemaphoreType.DMA((n,)),
            pltpu.SemaphoreType.DMA((n,)),
            pltpu.SemaphoreType.DMA((chunks * 4,)),
            pltpu.SemaphoreType.DMA((44,)),
            pltpu.SemaphoreType.DMA((2 * n,)),
            pltpu.SemaphoreType.DMA((1,)),
        ]
        + [pltpu.VMEM((n, tokens, LANES), bf16)] * (2 * chunks),
        compiler_params=pltpu.CompilerParams(
            collective_id=0, has_side_effects=True, vmem_limit_bytes=60 * 1024 * 1024
        ),
        cost_estimate=pl.CostEstimate(
            flops=8 * tacts * n * rows * tokens * features // n,
            bytes_accessed=400 * 1024 * 1024,
            transcendentals=0,
        ),
    )(ids, queries, goal_keys, goal_values, out_weight)


def direct_shards(n, queries, goal_keys, goal_values, out_weight, tactic_goal, tactic_len):
    tacts, rows, features = queries.shape
    ids = jnp.pad(tactic_goal.reshape(1, tacts), ((0, 7), (0, LANES - tacts)))
    context, weight = attend_exchange(n, ids, queries, goal_keys, goal_values, out_weight)
    weight = weight.reshape(features, out_weight.shape[1])
    projected = jnp.dot(
        context.reshape(tacts * rows, features), weight, preferred_element_type=jnp.float32
    )
    live_rows = (jnp.arange(rows)[None, :] < tactic_len[:, None]).reshape(tacts * rows, 1)
    projected = jnp.where(live_rows, projected, 0.0).astype(jnp.bfloat16)
    return projected.reshape(tacts, rows, weight.shape[1])


def solution(mesh):
    n = mesh.shape["goal"]

    def shards(queries, goal_keys, goal_values, out_weight, tactic_goal, tactic_len):
        fits = (
            n == 16 and mesh.shape["groups"] == 2
            and out_weight.shape[0] % 32 == 0
            and queries.shape[2] % (n * LANES) == 0
            and goal_keys.shape[0] == 1
            and queries.shape[0] <= LANES
        )
        body = functools.partial(direct_shards, n) if fits else plain_shards
        return body(queries, goal_keys, goal_values, out_weight, tactic_goal, tactic_len)

    return jax.shard_map(
        shards,
        mesh=mesh,
        in_specs=(
            P(("groups", "goal"), None, None),
            P(("groups", "goal"), None, None),
            P(("groups", "goal"), None, None),
            P("goal", None),
            P(("groups", "goal"), None),
            P(("groups", "goal")),
        ),
        out_specs=P(("groups", "goal"), None, None),
        check_vma=False,
    )
```
